32 devices in a mesh: groups: 2 (over x), dev: 16 (over z, y, core).
Axes of the slice: x: 2, y: 2, z: 4, core: 2. Of those that a mesh axis runs over, the one named last changes fastest.
Arguments:
- tokens: bfloat16 [64, 8192], P(('groups', 'dev')), parts along dimension 0, may hold values from -6 to 6
- gate_weight: bfloat16 [8192, 14336], P(None, 'dev'), may hold values from -0.0625 to 0.0625
- up_weight: bfloat16 [8192, 14336], P(None, 'dev'), may hold values from -0.0625 to 0.0625
- down_weight: bfloat16 [14336, 8192], P('dev'), may hold values from -0.0625 to 0.0625
- grad_in: bfloat16 [32, 14336, 32], P(('groups', 'dev')), parts along dimension 0, may hold values from -6 to 6
- grad_out: bfloat16 [32, 32, 8192], P(('groups', 'dev')), parts along dimension 0, may hold values from -6 to 6
- adapter_in: float32 [16, 14336, 32], P('groups', 'dev'), parts along dimension 0, may hold values from -6 to 6
- adapter_out: float32 [16, 32, 8192], P('groups', None, 'dev'), parts along dimension 0, may hold values from -6 to 6
- moment_in: float32 [16, 14336, 32], P('groups', 'dev'), parts along dimension 0, may hold values from -3 to 3
- moment_out: float32 [16, 32, 8192], P('groups', None, 'dev'), parts along dimension 0, may hold values from -3 to 3
- second_in: float32 [16, 14336, 32], P('groups', 'dev'), parts along dimension 0, may hold values from 0.001 to 0.1
- second_out: float32 [16, 32, 8192], P('groups', None, 'dev'), parts along dimension 0, may hold values from 0.001 to 0.1
- tenants: int32 [32], P('groups'), parts along dimension 0, may hold values from 0 to 7, never falling along the last dimension, each value on 1 to 8 neighbouring positions
- placement: int32 [32, 4], P('groups'), parts along dimension 0, may hold values from 0 to 7
- row_slot: int32 [64], P(('groups', 'dev')), parts along dimension 0, may hold values from 0 to 3
Outputs:
- layer_out: bfloat16 [64, 8192], P(('groups', 'dev')), parts along dimension 0
- new_in: float32 [16, 14336, 32], P('groups', 'dev'), parts along dimension 0
- new_out: float32 [16, 32, 8192], P('groups', None, 'dev'), parts along dimension 0
The draws below stay inside these ranges and needn't reach their ends.
There are 2 independent parts, one for each index of `groups`. The reference program is written for one: setup_inputs(seed, part) draws one part's arguments, and reference() takes and returns one part's arrays. A program takes and returns all parts, laid end to end along the dimension named above; an argument that names none is the same for every part. Nothing has to cross between parts.
Inputs may be any that keep to these rules, and one draw needn't show every extreme that they name: tenants never fall from one training device to the next; every adapter has 1 to 8 training devices, and one has exactly 8.
All inputs are finite; a program needn't handle non-finite values.
Results may differ from the reference program's by a relative error of at most 0.0062.
Values may be sent and summed in bfloat16 or wider, within the bound.
A program may use at most 192 MiB of HBM per device.

```python
import math
import jax
import jax.numpy as jnp
import numpy as np
from jax import lax

D = 8192
FFW = 14336
R = 32
MOST = 8
ROW_DEV = 2
WORKERS = 16
ADAPTERS = 8
SLOTS = 4
ROWS = 32


def with_ends(values, key, least, largest):
    spot = [jax.random.randint(jax.random.fold_in(key, axis), (), 0, length) for axis, length in enumerate(values.shape)]
    longest = values.shape.index(max(values.shape))
    beside = spot[:longest] + [(spot[longest] + 1) % values.shape[longest]] + spot[longest + 1:]
    return values.at[tuple(spot)].set(least).at[tuple(beside)].set(largest)


def raised(array, rng, source, target, shards_of, factor):
    owner, partner = [(jnp.arange(array.shape[dim]) // (array.shape[dim] // shards_of)).reshape([-1 if axis == dim else 1 for axis in range(array.ndim)]) for dim in (source, target)]
    chosen = jax.random.permutation(rng, shards_of)[partner]
    strong = (owner == chosen) | (owner == (partner + shards_of // 2) % shards_of)
    return jnp.where(strong, factor * array, array)


def block_levels(stream_key, dims, split, least, high):
    gain, own = 1.0, jax.random.fold_in(stream_key, 6)
    for position, shards_of in split:
        steps = jnp.exp(jax.random.uniform(jax.random.fold_in(own, position), (shards_of,), jnp.float32, least / len(split), high / len(split)))
        gain = gain * jnp.repeat(steps, dims[position] // shards_of).reshape([-1 if axis == position else 1 for axis in range(len(dims))])
    return gain


def split_up(count, total, most, slope):
    portions = [(1 << 20) // math.isqrt(grade ** slope) + 1 for grade in range(2, count + 1)]
    spare, given = total - most - (count - 1), [1] * (count - 1)
    while spare > 0:
        free = [i for i in range(count - 1) if given[i] < most]
        whole, left = sum([portions[i] for i in free]), spare
        for i in free:
            more = min(most - given[i], max(1, left * portions[i] // whole), spare)
            given[i] = given[i] + more
            spare = spare - more
    return np.array([most] + given)


def uneven_parts(own_key, amount, total, limit, slope):
    if amount == 2:
        one = jax.random.randint(own_key, (), max(1, total - limit), min(limit, total - 1) + 1)
        return jnp.stack([one, total - one])
    lengths = jnp.asarray(split_up(amount, total, limit, slope), jnp.int32)
    twos = (amount - 1) // 2
    giver, sink = lengths[1:1 + 2 * twos:2], lengths[2:2 + 2 * twos:2]
    slack = jnp.minimum(giver - 1, limit - sink)
    shifted = jax.random.randint(jax.random.fold_in(own_key, 1), (twos,), 0, 1 << 20) % (slack + 1)
    lengths = lengths.at[1:1 + 2 * twos:2].set(giver - shifted).at[2:2 + 2 * twos:2].set(sink + shifted)
    return lengths[jax.random.permutation(jax.random.fold_in(own_key, 2), amount)]


def normal_values(stream_key, dims, deviation, reach, split=(), held_as=jnp.bfloat16):
    gain = block_levels(stream_key, dims, split, -0.22, 0.18) if split else 1.0
    array = jax.random.normal(stream_key, dims, jnp.float32) * deviation * gain
    return jnp.minimum(jnp.maximum(array, -reach), reach).astype(held_as)


def noise_with(rng, dims, scale, limit, pieces, heavy, kind=jnp.bfloat16):
    result = scale * jax.random.normal(rng, dims, jnp.float32)
    if pieces:
        result = result * block_levels(rng, dims, pieces, -0.22, 0.18)
    return jnp.clip(raised(result, jax.random.fold_in(rng, 3), *heavy), -limit, limit).astype(kind)


def setup_inputs(seed: int = 0, part: int = 0) -> dict:
    arg_keys = jax.random.split(jax.random.key(seed), 16)
    part_splits = jax.random.split(jax.random.fold_in(arg_keys[15], part), 16)
    tokens = normal_values(part_splits[0], (ROWS, D), 1.0, 6.0, ((0, 16),))
    gate_weight = normal_values(arg_keys[1], (D, FFW), D ** -0.5, 0.0625, ((1, 16),))
    up_weight = normal_values(arg_keys[2], (D, FFW), D ** -0.5, 0.0625, ((1, 16),))
    down_weight = noise_with(arg_keys[3], (FFW, D), FFW ** -0.5, 0.0625, ((0, 16),), (0, 1, 16, 2.0))
    grad_in = normal_values(part_splits[4], (WORKERS, FFW, R), 1.0, 6.0, ((0, 16),))
    grad_out = normal_values(part_splits[5], (WORKERS, R, D), 1.0, 6.0, ((0, 16),))
    adapter_in = normal_values(part_splits[6], (ADAPTERS, FFW, R), 1.0, 6.0, ((1, 16),), jnp.float32)
    adapter_out = normal_values(part_splits[7], (ADAPTERS, R, D), 1.0, 6.0, ((2, 16),), jnp.float32)
    moment_in = normal_values(part_splits[8], (ADAPTERS, FFW, R), 0.5, 3.0, ((1, 16),), jnp.float32)
    moment_out = normal_values(part_splits[9], (ADAPTERS, R, D), 0.5, 3.0, ((2, 16),), jnp.float32)
    second_in = jnp.clip(jnp.exp(math.log(0.1) - 4.6051702 * jax.random.uniform(part_splits[10], (ADAPTERS, FFW, R), jnp.float32) ** block_levels(part_splits[10], (ADAPTERS, FFW, R), ((1, 16),), -0.2, 0.2)), 0.001, 0.1)
    second_out = jnp.clip(jnp.exp(math.log(0.1) - 4.6051702 * jax.random.uniform(part_splits[11], (ADAPTERS, R, D), jnp.float32) ** block_levels(part_splits[11], (ADAPTERS, R, D), ((2, 16),), -0.2, 0.2)), 0.001, 0.1)
    tenants = jnp.searchsorted(jnp.cumsum(uneven_parts(part_splits[12], ADAPTERS, WORKERS, MOST, 2)), jnp.arange(WORKERS), side="right").astype(jnp.int32)
    placement = with_ends(jax.random.randint(part_splits[13], (WORKERS, SLOTS), 0, ADAPTERS), jax.random.fold_in(part_splits[13], 1), 0, ADAPTERS - 1).astype(jnp.int32)
    row_slot = with_ends(jax.random.randint(part_splits[14], (ROWS,), 0, SLOTS), jax.random.fold_in(part_splits[14], 1), 0, SLOTS - 1).astype(jnp.int32)
    return dict(tokens=tokens, gate_weight=gate_weight, up_weight=up_weight, down_weight=down_weight, grad_in=grad_in, grad_out=grad_out, adapter_in=adapter_in, adapter_out=adapter_out, moment_in=moment_in, moment_out=moment_out, second_in=second_in, second_out=second_out, tenants=tenants, placement=placement, row_slot=row_slot)


first_decay = 0.9
second_decay = 0.999
learn_rate = 0.2
adam_eps = 1e-08
first_fix = 1.0 - 0.9 ** 10
second_fix = 1.0 - 0.999 ** 10

def adam_update(current, moment, second, gradient):
    moment_new = first_decay * moment + (1.0 - first_decay) * gradient
    second_new = second_decay * second + (1.0 - second_decay) * gradient * gradient
    return current - learn_rate * (moment_new / first_fix) / (jnp.sqrt(second_new / second_fix) + adam_eps)

def reference(tokens, gate_weight, up_weight, down_weight, grad_in, grad_out, adapter_in, adapter_out, moment_in, moment_out, second_in, second_out, tenants, placement, row_slot):
    owners = (tenants[None, :] == jnp.arange(ADAPTERS, dtype=jnp.int32)[:, None]).astype(jnp.float32)
    summed_in = jnp.einsum('an,nfk->afk', owners, grad_in.astype(jnp.float32), precision=lax.Precision.HIGHEST)
    summed_out = jnp.einsum('an,nkd->akd', owners, grad_out.astype(jnp.float32), precision=lax.Precision.HIGHEST)
    new_in = adam_update(adapter_in, moment_in, second_in, summed_in)
    new_out = adam_update(adapter_out, moment_out, second_out, summed_out)
    serve_in = new_in.astype(jnp.bfloat16)
    serve_out = new_out.astype(jnp.bfloat16)
    gate = jnp.dot(tokens, gate_weight, preferred_element_type=jnp.float32)
    upward = jnp.dot(tokens, up_weight, preferred_element_type=jnp.float32)
    hidden = (jax.nn.silu(gate) * upward).astype(jnp.bfloat16)
    base = jnp.dot(hidden, down_weight, preferred_element_type=jnp.float32)
    row_owner = jnp.arange(ROWS, dtype=jnp.int32) // ROW_DEV
    chosen = placement[row_owner, row_slot].astype(jnp.int32)
    picks = (chosen[:, None] == jnp.arange(ADAPTERS, dtype=jnp.int32)[None, :]).astype(jnp.float32)
    every = jnp.einsum('rf,afk->rak', hidden.astype(jnp.float32), serve_in.astype(jnp.float32))
    inner = lax.optimization_barrier(jnp.sum(every * picks[:, :, None], axis=1)) * (1.0 / math.sqrt(FFW))
    lifted = inner.astype(jnp.bfloat16)
    delta = jnp.einsum('rk,rkd->rd', lifted.astype(jnp.float32), serve_out[chosen].astype(jnp.float32))
    layer_out = (base + delta * (1.0 / math.sqrt(R))).astype(jnp.bfloat16)
    return (layer_out, new_in, new_out)
```

```python
import functools
import math

import jax
import jax.numpy as jnp
from jax import lax
from jax.experimental import pallas as pl
from jax.experimental.pallas import tpu as pltpu
from jax.sharding import PartitionSpec as P

FFW = 14336


first_decay = 0.9
second_decay = 0.999
learn_rate = 0.2
adam_eps = 1e-08
first_fix = 1.0 - 0.9**10
second_fix = 1.0 - 0.999**10


def adam_update(current, moment, second, gradient):
    moment_new = first_decay * moment + (1.0 - first_decay) * gradient
    second_new = second_decay * second + (1.0 - second_decay) * gradient * gradient
    return current - learn_rate * (moment_new / first_fix) / (
        jnp.sqrt(second_new / second_fix) + adam_eps
    )


def shards(
    tokens,
    gate_weight,
    up_weight,
    down_weight,
    grad_in,
    grad_out,
    adapter_in,
    adapter_out,
    moment_in,
    moment_out,
    second_in,
    second_out,
    tenants,
    placement,
    row_slot,
):
    workers = lax.axis_size("dev")
    device_index = lax.axis_index("dev")
    adapter_count = adapter_in.shape[0]
    hidden_block = adapter_in.shape[1]
    adapter_rank = adapter_in.shape[2]
    column_block = adapter_out.shape[2]
    slot_count = placement.shape[1]
    inv_rank = 1.0 / math.sqrt(adapter_rank)
    flat_in = grad_in.reshape(1, workers, hidden_block * adapter_rank)
    flat_out = grad_out.reshape(adapter_rank, workers, column_block)
    got_in, got_out = (
        lax.all_to_all(flat_in, "dev", split_axis=1, concat_axis=1, tiled=True),
        lax.all_to_all(flat_out, "dev", split_axis=1, concat_axis=1, tiled=True),
    )
    owners = (tenants[None, :] == jnp.arange(adapter_count, dtype=jnp.int32)[:, None]).astype(
        jnp.bfloat16
    )
    summed_in = jnp.einsum(
        "an,nk->ak", owners, got_in[0], preferred_element_type=jnp.float32
    ).reshape(adapter_count, hidden_block, adapter_rank)
    summed_out = jnp.einsum("an,knc->akc", owners, got_out, preferred_element_type=jnp.float32)
    new_in = adam_update(adapter_in, moment_in, second_in, summed_in)
    new_out = adam_update(adapter_out, moment_out, second_out, summed_out)
    serve_in = new_in.astype(jnp.bfloat16)
    serve_out = new_out.astype(jnp.bfloat16)
    chosen_own = placement[device_index][row_slot]
    hot_own = (chosen_own[:, None] == jnp.arange(adapter_count, dtype=jnp.int32)[None, :]).astype(
        jnp.bfloat16
    )
    all_tokens, hot_all = (
        lax.all_gather(tokens, "dev", axis=0, tiled=True),
        lax.all_gather(hot_own, "dev", axis=0, tiled=True),
    )
    gate = jnp.dot(all_tokens, gate_weight, preferred_element_type=jnp.float32)
    upward = jnp.dot(all_tokens, up_weight, preferred_element_type=jnp.float32)
    hidden = (jax.nn.silu(gate) * upward).astype(jnp.bfloat16)
    every = jnp.einsum("rf,afk->rak", hidden, serve_in, preferred_element_type=jnp.float32)
    inner_part = jnp.sum(every * hot_all.astype(jnp.float32)[:, :, None], axis=1) * (
        1.0 / math.sqrt(FFW)
    )
    lifted = lax.psum_scatter(inner_part, "dev", scatter_dimension=0, tiled=True).astype(
        jnp.bfloat16
    )
    partial_sum = jnp.dot(hidden, down_weight, preferred_element_type=jnp.float32)
    summed_rows = lax.psum_scatter(partial_sum, "dev", scatter_dimension=0, tiled=True)
    outgoing = serve_out[placement]
    arrived = lax.all_to_all(outgoing, "dev", split_axis=0, concat_axis=3, tiled=True)
    slot_pick = (row_slot[:, None] == jnp.arange(slot_count, dtype=jnp.int32)[None, :]).astype(
        jnp.float32
    )
    delta_every = jnp.einsum("rk,skd->rsd", lifted, arrived[0], preferred_element_type=jnp.float32)
    delta = jnp.sum(delta_every * slot_pick[:, :, None], axis=1)
    layer_out = (summed_rows + delta * inv_rank).astype(jnp.bfloat16)
    return (layer_out, new_in, new_out)


MESH = pl.DeviceIdType.MESH
CHUNKS = 8


def fused_kernel(
    n,
    payload,
    gate,
    up,
    down,
    grad_in,
    grad_out,
    adapter_in,
    moment_in,
    second_in,
    adapter_out,
    moment_out,
    second_out,
    owners,
    layer,
    new_in,
    new_out,
    gate_s,
    up_s,
    down_s,
    tok_s,
    gin_s,
    gout_s,
    ad_in,
    ad_out,
    new_in_s,
    new_out_s,
    serve_in,
    serve_out,
    accg,
    accu,
    part,
    own,
    got_part,
    got_inner,
    rows_out,
    got_rows,
    weight_sem,
    local_sem,
    tok_send,
    tok_recv,
    gin_send,
    gin_recv,
    gout_send,
    gout_recv,
    part_send,
    part_recv,
    inner_send,
    inner_recv,
    rows_send,
    rows_recv,
):
    me = lax.axis_index("dev")
    adapters, rank, hidden_block = ad_in.shape[1:]
    column_block = ad_out.shape[3]
    lanes = adapters * rank
    width = payload.shape[1] - 128
    depth = gate_s.shape[1]
    row_count = accg.shape[0]

    def other(s):
        return lax.rem(me + s, n)

    def remote(src, dst, send, recv, peer):
        return pltpu.make_async_remote_copy(
            src_ref=src,
            dst_ref=dst,
            send_sem=send,
            recv_sem=recv,
            device_id={"dev": peer},
            device_id_type=MESH,
        )

    def each(body):
        def step(s, carry):
            body(other(s))
            return carry

        lax.fori_loop(1, n, step, 0)

    def hid(j):
        return pl.ds(pl.multiple_of(j * hidden_block, 128), hidden_block)

    def col(j):
        return pl.ds(pl.multiple_of(j * column_block, 128), column_block)

    def send_tok(p):
        return remote(payload, tok_s.at[me], tok_send.at[p], tok_recv.at[me], p)

    def send_gin(p):
        return remote(
            grad_in.at[:, hid(p)], gin_s.at[me], gin_send.at[p], gin_recv.at[me], p
        )

    def send_gout(p):
        return remote(
            grad_out.at[:, col(p)], gout_s.at[me], gout_send.at[p], gout_recv.at[me], p
        )

    def send_part(p):
        return remote(part.at[p], got_part.at[me], part_send.at[p], part_recv.at[me], p)

    def send_inner(p):
        return remote(
            got_inner.at[me], got_inner.at[me], inner_send.at[p], inner_recv.at[me], p
        )

    def send_rows(p):
        return remote(rows_out.at[p], got_rows.at[me], rows_send.at[p], rows_recv.at[me], p)

    def arrived(buf, send, recv):
        each(lambda p: remote(buf.at[p], buf.at[p], send.at[p], recv.at[p], p).wait_recv())

    def gate_copy(c):
        rows = pl.ds(pl.multiple_of(c * depth, 128), depth)
        return pltpu.make_async_copy(gate.at[rows, :], gate_s.at[c], weight_sem.at[c])

    def up_copy(c):
        rows = pl.ds(pl.multiple_of(c * depth, 128), depth)
        return pltpu.make_async_copy(up.at[rows, :], up_s.at[c], weight_sem.at[CHUNKS + c])

    def down_copy(s):
        return pltpu.make_async_copy(
            down.at[:, col(other(s))], down_s.at[s], weight_sem.at[2 * CHUNKS + s]
        )

    own_tok = pltpu.make_async_copy(payload, tok_s.at[me], local_sem.at[0])
    own_gin = pltpu.make_async_copy(grad_in.at[:, hid(me)], gin_s.at[me], local_sem.at[1])
    own_gout = pltpu.make_async_copy(grad_out.at[:, col(me)], gout_s.at[me], local_sem.at[2])
    loads = [
        pltpu.make_async_copy(ref, dst, local_sem.at[3 + i])
        for i, (ref, dst) in enumerate(
            [
                (adapter_in, ad_in.at[0]),
                (moment_in, ad_in.at[1]),
                (second_in, ad_in.at[2]),
                (adapter_out, ad_out.at[0]),
                (moment_out, ad_out.at[1]),
                (second_out, ad_out.at[2]),
            ]
        )
    ]
    store_in = pltpu.make_async_copy(new_in_s, new_in, local_sem.at[9])
    store_out = pltpu.make_async_copy(new_out_s, new_out, local_sem.at[10])

    barrier = pltpu.get_barrier_semaphore()
    each(
        lambda p: pl.semaphore_signal(
            barrier, inc=1, device_id={"dev": p}, device_id_type=MESH
        )
    )
    own_tok.start()

    def start_weights(c, carry):
        gate_copy(c).start()
        up_copy(c).start()
        return carry

    lax.fori_loop(0, CHUNKS, start_weights, 0)
    pl.semaphore_wait(barrier, n - 1)
    each(lambda p: send_tok(p).start())
    each(lambda p: send_gout(p).start())
    each(lambda p: send_gin(p).start())
    own_gin.start()
    own_gout.start()

    def start_down(s, carry):
        down_copy(lax.rem(s + 1, n)).start()
        return carry

    lax.fori_loop(0, n, start_down, 0)
    for load in loads:
        load.start()

    accg[...] = jnp.zeros_like(accg)
    accu[...] = jnp.zeros_like(accu)
    own_tok.wait()
    arrived(tok_s, tok_send, tok_recv)

    packed = n * tok_s.shape[1]
    shift = lax.broadcasted_iota(jnp.int32, (row_count, packed), 1) - (
        CHUNKS * lax.broadcasted_iota(jnp.int32, (row_count, packed), 0)
    )

    def pick(c):
        return jnp.where(shift == c, 1.0, 0.0).astype(jnp.bfloat16)

    def project(c, carry):
        tokens = tok_s[:, :, :width].reshape(packed, width)
        block = jnp.dot(pick(c), tokens, preferred_element_type=jnp.float32).astype(
            jnp.bfloat16
        )
        gate_copy(c).wait()
        accg[...] += jnp.dot(block, gate_s[c], preferred_element_type=jnp.float32)
        up_copy(c).wait()
        accu[...] += jnp.dot(block, up_s[c], preferred_element_type=jnp.float32)
        return carry

    lax.fori_loop(0, CHUNKS, project, 0)
    hot = jnp.dot(
        pick(0),
        tok_s[:, :, width:].reshape(packed, 128),
        preferred_element_type=jnp.float32,
    ).astype(jnp.bfloat16)
    spread = jnp.where(
        lax.broadcasted_iota(jnp.int32, (128, lanes), 1) // rank
        == lax.broadcasted_iota(jnp.int32, (128, lanes), 0),
        1.0,
        0.0,
    ).astype(jnp.bfloat16)
    mask = jnp.dot(hot, spread, preferred_element_type=jnp.float32)
    gated = accg[...]
    hidden = (gated / (1.0 + jnp.exp(-gated)) * accu[...]).astype(jnp.bfloat16)

    def project_down(s, carry):
        p = other(s)
        down_copy(s).wait()
        part[p] = jnp.dot(hidden, down_s[s], preferred_element_type=jnp.float32).astype(
            jnp.bfloat16
        )
        send_part(p).start()
        return carry

    lax.fori_loop(1, n, project_down, 0)
    down_copy(0).wait()
    own[...] = jnp.dot(hidden, down_s[0], preferred_element_type=jnp.float32)

    def update(got, state, new_s, serve):
        def block(i, carry):
            rows = pl.ds(pl.multiple_of(lax.rem(i, rank // 16) * 16, 16), 16)
            cols = pl.ds(pl.multiple_of(lax.div(i, rank // 16) * 128, 128), 128)
            grads = [got[k, rows, cols].astype(jnp.float32) for k in range(n)]
            for a in range(adapters):
                total = owners[a * n : a * n + 1, :] * grads[0]
                for k in range(1, n):
                    total += owners[a * n + k : a * n + k + 1, :] * grads[k]
                first = first_decay * state[1, a, rows, cols] + (1.0 - first_decay) * total
                second = (
                    second_decay * state[2, a, rows, cols]
                    + (1.0 - second_decay) * total * total
                )
                value = state[0, a, rows, cols] - (learn_rate / first_fix) * first / (
                    jnp.sqrt(second * (1.0 / second_fix)) + adam_eps
                )
                new_s[a, rows, cols] = value
                at = pl.ds(pl.multiple_of(a * rank + lax.rem(i, rank // 16) * 16, 16), 16)
                serve[at, cols] = value.astype(jnp.bfloat16)
            return carry

        lax.fori_loop(0, (rank // 16) * (got.shape[2] // 128), block, 0)

    for load in loads:
        load.wait()
    own_gout.wait()
    arrived(gout_s, gout_send, gout_recv)
    update(gout_s, ad_out, new_out_s, serve_out)
    store_out.start()
    own_gin.wait()
    arrived(gin_s, gin_send, gin_recv)
    update(gin_s, ad_in, new_in_s, serve_in)
    store_in.start()

    every = lax.dot_general(
        hidden, serve_in[...], (((1,), (1,)), ((), ())), preferred_element_type=jnp.float32
    )
    every = every * mask
    inner = every[:, :128]
    for q in range(1, lanes // 128):
        inner += every[:, 128 * q : 128 * q + 128]
    turn = 128
    while turn > rank:
        turn //= 2
        inner += pltpu.roll(inner, turn, 1)
    group = lax.broadcasted_iota(jnp.int32, (8, 128), 1) // rank
    folded = jnp.zeros((8, 128), jnp.float32)
    for q in range(row_count // 8):
        folded += jnp.where(group == q, inner[8 * q : 8 * q + 8, :], 0.0)
    got_inner[me] = folded
    each(lambda p: send_inner(p).start())

    arrived(got_part, part_send, part_recv)

    def add_part(s, carry):
        own[...] += got_part[other(s)].astype(jnp.float32)
        return carry

    lax.fori_loop(1, n, add_part, 0)

    arrived(got_inner, inner_send, inner_recv)
    inner_sum = got_inner[0]
    for k in range(1, n):
        inner_sum += got_inner[k]
    inner_sum = inner_sum * (1.0 / math.sqrt(FFW))
    pieces = []
    for q in range(row_count // 8):
        piece = jnp.where(group == q, inner_sum, 0.0)
        turn = 128
        while turn > rank:
            turn //= 2
            piece += pltpu.roll(piece, turn, 1)
        pieces.append(piece)
    lifted = jnp.concatenate(pieces, axis=0)
    lifted = jnp.concatenate([lifted] * (lanes // 128), axis=1)
    lifted = (lifted * mask).astype(jnp.bfloat16)
    delta = jnp.dot(lifted, serve_out[...], preferred_element_type=jnp.float32)
    result = own[...] + delta * (1.0 / math.sqrt(rank))
    per = row_count // n
    for j in range(n):
        rows_out[j] = result[per * j : per * j + per, :]
    each(lambda p: send_rows(p).start())
    got_rows[me] = rows_out[me]
    each(lambda p: send_tok(p).wait_send())
    each(lambda p: send_gin(p).wait_send())
    each(lambda p: send_gout(p).wait_send())
    each(lambda p: send_part(p).wait_send())
    each(lambda p: send_inner(p).wait_send())
    store_in.wait()
    store_out.wait()
    arrived(got_rows, rows_send, rows_recv)
    for j in range(n):
        layer[:, column_block * j : column_block * (j + 1)] = got_rows[j].astype(jnp.bfloat16)
    each(lambda p: send_rows(p).wait_send())


def fused_shards(
    tokens,
    gate_weight,
    up_weight,
    down_weight,
    grad_in,
    grad_out,
    adapter_in,
    adapter_out,
    moment_in,
    moment_out,
    second_in,
    second_out,
    tenants,
    placement,
    row_slot,
):
    n = lax.axis_size("dev")
    me = lax.axis_index("dev")
    per, model = tokens.shape
    adapters, hidden_block, rank = adapter_in.shape
    column_block = adapter_out.shape[2]
    slots = placement.shape[1]
    rows = n * per
    width = model // CHUNKS
    lanes = adapters * rank
    code = jnp.arange(adapters, dtype=jnp.int32)
    owners = (tenants[None, :] == code[:, None]).astype(jnp.float32).reshape(adapters * n, 1)
    owners = jnp.broadcast_to(owners, (adapters * n, 128))
    mine = (jnp.arange(n, dtype=jnp.int32) == me)[None, :, None, None]
    slot = (row_slot[:, None] == jnp.arange(slots, dtype=jnp.int32)[None, :])[:, None, :, None]
    held = placement[None, :, :, None] == jnp.arange(128, dtype=jnp.int32)[None, None, None, :]
    hot = jnp.any(mine & slot & held, axis=(1, 2)).astype(jnp.bfloat16)
    hot = jnp.broadcast_to(hot[:, None, :], (per, CHUNKS, 128)).reshape(per * CHUNKS, 128)
    payload = jnp.concatenate([tokens.reshape(per * CHUNKS, width), hot], axis=1)
    dma = pltpu.SemaphoreType.DMA
    bf16, f32 = jnp.bfloat16, jnp.float32
    vmem, hbm = pl.BlockSpec(memory_space=pltpu.VMEM), pl.BlockSpec(memory_space=pl.ANY)
    layer, new_in, new_out = pl.pallas_call(
        functools.partial(fused_kernel, n),
        out_shape=(
            jax.ShapeDtypeStruct((per, model), bf16),
            jax.ShapeDtypeStruct((adapters, rank, hidden_block), f32),
            jax.ShapeDtypeStruct((adapters, rank, column_block), f32),
        ),
        in_specs=[hbm] * 12 + [vmem],
        out_specs=(vmem, hbm, hbm),
        scratch_shapes=[
            pltpu.VMEM((CHUNKS, width, hidden_block), bf16),
            pltpu.VMEM((CHUNKS, width, hidden_block), bf16),
            pltpu.VMEM((n, hidden_block, column_block), bf16),
            pltpu.VMEM((n, per * CHUNKS, width + 128), bf16),
            pltpu.VMEM((n, rank, hidden_block), bf16),
            pltpu.VMEM((n, rank, column_block), bf16),
            pltpu.VMEM((3, adapters, rank, hidden_block), f32),
            pltpu.VMEM((3, adapters, rank, column_block), f32),
            pltpu.VMEM((adapters, rank, hidden_block), f32),
            pltpu.VMEM((adapters, rank, column_block), f32),
            pltpu.VMEM((lanes, hidden_block), bf16),
            pltpu.VMEM((lanes, column_block), bf16),
            pltpu.VMEM((rows, hidden_block), f32),
            pltpu.VMEM((rows, hidden_block), f32),
            pltpu.VMEM((n, rows, column_block), bf16),
            pltpu.VMEM((rows, column_block), f32),
            pltpu.VMEM((n, rows, column_block), bf16),
            pltpu.VMEM((n, 8, 128), f32),
            pltpu.VMEM((n, per, column_block), f32),
            pltpu.VMEM((n, per, column_block), f32),
            dma((2 * CHUNKS + n,)),
            dma((11,)),
        ]
        + [dma((n,))] * 12,
        compiler_params=pltpu.CompilerParams(
            collective_id=0, has_side_effects=True, vmem_limit_bytes=60 * 1024 * 1024
        ),
    )(
        payload,
        gate_weight,
        up_weight,
        down_weight,
        jnp.swapaxes(grad_in[0], 0, 1),
        grad_out[0],
        jnp.swapaxes(adapter_in, 1, 2),
        jnp.swapaxes(moment_in, 1, 2),
        jnp.swapaxes(second_in, 1, 2),
        adapter_out,
        moment_out,
        second_out,
        owners,
    )
    return layer, jnp.swapaxes(new_in, 1, 2), new_out


def fits(mesh, tokens, adapter_in, adapter_out):
    n = mesh.shape["dev"]
    per = tokens.shape[0] // (n * mesh.shape["groups"])
    adapters = adapter_in.shape[0] // mesh.shape["groups"]
    rank = adapter_in.shape[2]
    return (
        (adapter_in.shape[1] // n) % 128 == 0
        and (adapter_out.shape[2] // n) % 128 == 0
        and per * CHUNKS == 16
        and tokens.shape[1] % (CHUNKS * 128) == 0
        and 128 % rank == 0
        and rank % 16 == 0
        and adapters <= 128
        and (adapters * rank) % 128 == 0
        and n * per == 8 * (128 // rank)
    )


def solution(mesh):
    in_specs = (
        P(("groups", "dev"), None),
        P(None, "dev"),
        P(None, "dev"),
        P("dev", None),
        P(("groups", "dev"), None, None),
        P(("groups", "dev"), None, None),
        P("groups", "dev", None),
        P("groups", None, "dev"),
        P("groups", "dev", None),
        P("groups", None, "dev"),
        P("groups", "dev", None),
        P("groups", None, "dev"),
        P("groups"),
        P("groups", None),
        P(("groups", "dev")),
    )
    out_specs = (P(("groups", "dev"), None), P("groups", "dev", None), P("groups", None, "dev"))

    def program(*args):
        body = fused_shards if fits(mesh, args[0], args[6], args[7]) else shards
        return jax.shard_map(
            body, mesh=mesh, in_specs=in_specs, out_specs=out_specs, check_vma=False
        )(*args)

    return program
```

```python
import functools
import math

import jax
import jax.numpy as jnp
from jax import lax
from jax.experimental import pallas as pl
from jax.experimental.pallas import tpu as pltpu
from jax.sharding import PartitionSpec as P

FFW = 14336


first_decay = 0.9
second_decay = 0.999
learn_rate = 0.2
adam_eps = 1e-08
first_fix = 1.0 - 0.9**10
second_fix = 1.0 - 0.999**10


def adam_update(current, moment, second, gradient):
    moment_new = first_decay * moment + (1.0 - first_decay) * gradient
    second_new = second_decay * second + (1.0 - second_decay) * gradient * gradient
    return current - learn_rate * (moment_new / first_fix) / (
        jnp.sqrt(second_new / second_fix) + adam_eps
    )


def shards(
    tokens,
    gate_weight,
    up_weight,
    down_weight,
    grad_in,
    grad_out,
    adapter_in,
    adapter_out,
    moment_in,
    moment_out,
    second_in,
    second_out,
    tenants,
    placement,
    row_slot,
):
    workers = lax.axis_size("dev")
    device_index = lax.axis_index("dev")
    adapter_count = adapter_in.shape[0]
    hidden_block = adapter_in.shape[1]
    adapter_rank = adapter_in.shape[2]
    column_block = adapter_out.shape[2]
    slot_count = placement.shape[1]
    inv_rank = 1.0 / math.sqrt(adapter_rank)
    flat_in = grad_in.reshape(1, workers, hidden_block * adapter_rank)
    flat_out = grad_out.reshape(adapter_rank, workers, column_block)
    got_in, got_out = (
        lax.all_to_all(flat_in, "dev", split_axis=1, concat_axis=1, tiled=True),
        lax.all_to_all(flat_out, "dev", split_axis=1, concat_axis=1, tiled=True),
    )
    owners = (tenants[None, :] == jnp.arange(adapter_count, dtype=jnp.int32)[:, None]).astype(
        jnp.bfloat16
    )
    summed_in = jnp.einsum(
        "an,nk->ak", owners, got_in[0], preferred_element_type=jnp.float32
    ).reshape(adapter_count, hidden_block, adapter_rank)
    summed_out = jnp.einsum("an,knc->akc", owners, got_out, preferred_element_type=jnp.float32)
    new_in = adam_update(adapter_in, moment_in, second_in, summed_in)
    new_out = adam_update(adapter_out, moment_out, second_out, summed_out)
    serve_in = new_in.astype(jnp.bfloat16)
    serve_out = new_out.astype(jnp.bfloat16)
    chosen_own = placement[device_index][row_slot]
    hot_own = (chosen_own[:, None] == jnp.arange(adapter_count, dtype=jnp.int32)[None, :]).astype(
        jnp.bfloat16
    )
    all_tokens, hot_all = (
        lax.all_gather(tokens, "dev", axis=0, tiled=True),
        lax.all_gather(hot_own, "dev", axis=0, tiled=True),
    )
    gate = jnp.dot(all_tokens, gate_weight, preferred_element_type=jnp.float32)
    upward = jnp.dot(all_tokens, up_weight, preferred_element_type=jnp.float32)
    hidden = (jax.nn.silu(gate) * upward).astype(jnp.bfloat16)
    every = jnp.einsum("rf,afk->rak", hidden, serve_in, preferred_element_type=jnp.float32)
    inner_part = jnp.sum(every * hot_all.astype(jnp.float32)[:, :, None], axis=1) * (
        1.0 / math.sqrt(FFW)
    )
    lifted = lax.psum_scatter(inner_part, "dev", scatter_dimension=0, tiled=True).astype(
        jnp.bfloat16
    )
    partial_sum = jnp.dot(hidden, down_weight, preferred_element_type=jnp.float32)
    summed_rows = lax.psum_scatter(partial_sum, "dev", scatter_dimension=0, tiled=True)
    outgoing = serve_out[placement]
    arrived = lax.all_to_all(outgoing, "dev", split_axis=0, concat_axis=3, tiled=True)
    slot_pick = (row_slot[:, None] == jnp.arange(slot_count, dtype=jnp.int32)[None, :]).astype(
        jnp.float32
    )
    delta_every = jnp.einsum("rk,skd->rsd", lifted, arrived[0], preferred_element_type=jnp.float32)
    delta = jnp.sum(delta_every * slot_pick[:, :, None], axis=1)
    layer_out = (summed_rows + delta * inv_rank).astype(jnp.bfloat16)
    return (layer_out, new_in, new_out)


MESH = pl.DeviceIdType.MESH
CHUNKS = 8


def fused_kernel(
    n,
    tokens,
    tenants,
    placement,
    row_slot,
    gate,
    up,
    down,
    grad_in,
    grad_out,
    adapter_in,
    moment_in,
    second_in,
    adapter_out,
    moment_out,
    second_out,
    layer,
    new_in,
    new_out,
    gate_s,
    up_s,
    down_s,
    tok_s,
    gin_s,
    gout_s,
    ad_in,
    ad_out,
    new_in_s,
    new_out_s,
    serve_in,
    serve_out,
    accg,
    accu,
    mate_part,
    got_mate,
    part,
    own,
    got_part,
    owners,
    payload,
    got_inner,
    rows_out,
    got_rows,
    weight_sem,
    local_sem,
    tok_send,
    tok_recv,
    gin_send,
    gin_recv,
    gout_send,
    gout_recv,
    relay_send,
    mate_send,
    mate_recv,
    part_send,
    part_recv,
    inner_send,
    inner_recv,
    rows_send,
    rows_recv,
):
    me = lax.axis_index("dev")
    adapters, rank, hidden_block = ad_in.shape[1:]
    column_block = ad_out.shape[3]
    lanes = adapters * rank
    width = tok_s.shape[2] - 128
    depth = gate_s.shape[1]
    row_count = accg.shape[0]

    core = lax.rem(me, 2)
    mate = me + 1 - 2 * core
    half = n // 2

    def other(s):
        return lax.rem(me + s, n)

    def chip(s):
        return lax.rem(me + 2 * s, n)

    def across(s):
        return lax.rem(mate + 2 * s, n)

    def remote(src, dst, send, recv, peer):
        return pltpu.make_async_remote_copy(
            src_ref=src,
            dst_ref=dst,
            send_sem=send,
            recv_sem=recv,
            device_id={"dev": peer},
            device_id_type=MESH,
        )

    def each(body):
        def step(s, carry):
            body(other(s))
            return carry

        lax.fori_loop(1, n, step, 0)

    def each_chip(body):
        def step(s, carry):
            body(chip(s))
            return carry

        lax.fori_loop(1, half, step, 0)

    def hid(j):
        return pl.ds(pl.multiple_of(j * hidden_block, 128), hidden_block)

    def col(j):
        return pl.ds(pl.multiple_of(j * column_block, 128), column_block)

    def send_tok(p):
        return remote(tok_s.at[me], tok_s.at[me], tok_send.at[p], tok_recv.at[me], p)

    def relay(p):
        return remote(tok_s.at[p], tok_s.at[p], relay_send.at[p], tok_recv.at[p], mate)

    def tok_arrived(p):
        return remote(tok_s.at[p], tok_s.at[p], tok_send.at[p], tok_recv.at[p], p)

    def send_mate(s):
        return remote(
            mate_part.at[s], got_mate.at[s], mate_send.at[s], mate_recv.at[s], mate
        )

    def send_gin(p):
        return remote(
            grad_in.at[:, hid(p)], gin_s.at[me], gin_send.at[p], gin_recv.at[me], p
        )

    def send_gout(p):
        return remote(
            grad_out.at[:, col(p)], gout_s.at[me], gout_send.at[p], gout_recv.at[me], p
        )

    def send_part(p):
        return remote(part.at[p], got_part.at[me], part_send.at[p], part_recv.at[me], p)

    def send_inner(p):
        return remote(
            got_inner.at[me], got_inner.at[me], inner_send.at[p], inner_recv.at[me], p
        )

    def send_rows(p):
        return remote(rows_out.at[p], got_rows.at[me], rows_send.at[p], rows_recv.at[me], p)

    def arrived(buf, send, recv):
        each(lambda p: remote(buf.at[p], buf.at[p], send.at[p], recv.at[p], p).wait_recv())

    def gate_copy(c):
        rows = pl.ds(pl.multiple_of(c * depth, 128), depth)
        return pltpu.make_async_copy(gate.at[rows, :], gate_s.at[c], weight_sem.at[c])

    def up_copy(c):
        rows = pl.ds(pl.multiple_of(c * depth, 128), depth)
        return pltpu.make_async_copy(up.at[rows, :], up_s.at[c], weight_sem.at[CHUNKS + c])

    def down_copy(s, p):
        return pltpu.make_async_copy(
            down.at[:, col(p)], down_s.at[s], weight_sem.at[2 * CHUNKS + s]
        )

    own_gin = pltpu.make_async_copy(grad_in.at[:, hid(me)], gin_s.at[me], local_sem.at[1])
    own_gout = pltpu.make_async_copy(grad_out.at[:, col(me)], gout_s.at[me], local_sem.at[2])
    loads = [
        pltpu.make_async_copy(ref, dst, local_sem.at[3 + i])
        for i, (ref, dst) in enumerate(
            [
                (adapter_in, ad_in.at[0]),
                (moment_in, ad_in.at[1]),
                (second_in, ad_in.at[2]),
                (adapter_out, ad_out.at[0]),
                (moment_out, ad_out.at[1]),
                (second_out, ad_out.at[2]),
            ]
        )
    ]
    store_in = pltpu.make_async_copy(new_in_s, new_in, local_sem.at[9])
    store_out = pltpu.make_async_copy(new_out_s, new_out, local_sem.at[10])

    barrier = pltpu.get_barrier_semaphore()
    each(
        lambda p: pl.semaphore_signal(
            barrier, inc=1, device_id={"dev": p}, device_id_type=MESH
        )
    )

    def start_weights(c, carry):
        gate_copy(c).start()
        up_copy(c).start()
        return carry

    lax.fori_loop(0, CHUNKS, start_weights, 0)
    values = tokens[...].astype(jnp.float32)
    lane = lax.broadcasted_iota(jnp.int32, (CHUNKS, 128), 1)
    for r in range(row_count // n):
        for c in range(CHUNKS):
            payload[r * CHUNKS + c : r * CHUNKS + c + 1, :width] = values[
                r : r + 1, c * width : (c + 1) * width
            ]
        chosen = placement[row_slot[r], me]
        payload[r * CHUNKS : (r + 1) * CHUNKS, width:] = jnp.where(lane == chosen, 1.0, 0.0)
    tok_s[me] = payload[...].astype(jnp.bfloat16)
    pl.semaphore_wait(barrier, n - 1)
    send_tok(mate).start()
    each_chip(lambda p: send_tok(p).start())
    each(lambda p: send_gin(p).start())
    each(lambda p: send_gout(p).start())
    own_gin.start()
    own_gout.start()

    def start_across(s, carry):
        down_copy(s, across(s)).start()
        return carry

    def start_chip(s, carry):
        down_copy(half + s, chip(s)).start()
        return carry

    lax.fori_loop(0, half, start_across, 0)
    lax.fori_loop(0, half, start_chip, 0)
    for load in loads:
        load.start()

    accg[...] = jnp.zeros_like(accg)
    accu[...] = jnp.zeros_like(accu)
    code = lax.broadcasted_iota(jnp.int32, (adapters, 128), 0)
    for k in range(n):
        owners[k * adapters : (k + 1) * adapters, :] = jnp.where(code == tenants[k], 1.0, 0.0)

    def pass_on(p):
        tok_arrived(p).wait_recv()
        relay(p).start()

    each_chip(pass_on)
    tok_arrived(mate).wait_recv()

    def relayed(s, carry):
        tok_arrived(across(s)).wait_recv()
        return carry

    lax.fori_loop(1, half, relayed, 0)

    packed = n * tok_s.shape[1]
    shift = lax.broadcasted_iota(jnp.int32, (row_count, packed), 1) - (
        CHUNKS * lax.broadcasted_iota(jnp.int32, (row_count, packed), 0)
    )

    def pick(c):
        return jnp.where(shift == c, 1.0, 0.0).astype(jnp.bfloat16)

    def project(c, carry):
        tokens = tok_s[:, :, :width].reshape(packed, width)
        block = jnp.dot(pick(c), tokens, preferred_element_type=jnp.float32).astype(
            jnp.bfloat16
        )
        gate_copy(c).wait()
        accg[...] += jnp.dot(block, gate_s[c], preferred_element_type=jnp.float32)
        up_copy(c).wait()
        accu[...] += jnp.dot(block, up_s[c], preferred_element_type=jnp.float32)
        return carry

    lax.fori_loop(0, CHUNKS, project, 0)
    hot = jnp.dot(
        pick(0),
        tok_s[:, :, width:].reshape(packed, 128),
        preferred_element_type=jnp.float32,
    ).astype(jnp.bfloat16)
    spread = jnp.where(
        lax.broadcasted_iota(jnp.int32, (128, lanes), 1) // rank
        == lax.broadcasted_iota(jnp.int32, (128, lanes), 0),
        1.0,
        0.0,
    ).astype(jnp.bfloat16)
    mask = jnp.dot(hot, spread, preferred_element_type=jnp.float32)
    gated = accg[...]
    hidden = (gated / (1.0 + jnp.exp(-gated)) * accu[...]).astype(jnp.bfloat16)

    def down_across(s, carry):
        down_copy(s, across(s)).wait()
        mate_part[s] = jnp.dot(hidden, down_s[s], preferred_element_type=jnp.float32)
        send_mate(s).start()
        return carry

    lax.fori_loop(0, half, down_across, 0)

    def down_chip(s, carry):
        p = chip(s)
        down_copy(half + s, p).wait()
        whole = jnp.dot(hidden, down_s[half + s], preferred_element_type=jnp.float32)
        send_mate(s).wait_recv()
        part[p] = (whole + got_mate[s]).astype(jnp.bfloat16)
        send_part(p).start()
        return carry

    lax.fori_loop(1, half, down_chip, 0)
    down_copy(half, me).wait()
    send_mate(0).wait_recv()
    own[...] = got_mate[0] + jnp.dot(
        hidden, down_s[half], preferred_element_type=jnp.float32
    )

    def update(got, state, new_s, serve):
        def block(i, carry):
            rows = pl.ds(pl.multiple_of(lax.rem(i, rank // 16) * 16, 16), 16)
            cols = pl.ds(pl.multiple_of(lax.div(i, rank // 16) * 128, 128), 128)
            grads = [got[k, rows, cols].astype(jnp.float32) for k in range(n)]
            for a in range(adapters):
                total = owners[a : a + 1, :] * grads[0]
                for k in range(1, n):
                    total += owners[k * adapters + a : k * adapters + a + 1, :] * grads[k]
                first = first_decay * state[1, a, rows, cols] + (1.0 - first_decay) * total
                second = (
                    second_decay * state[2, a, rows, cols]
                    + (1.0 - second_decay) * total * total
                )
                value = state[0, a, rows, cols] - (learn_rate / first_fix) * first / (
                    jnp.sqrt(second * (1.0 / second_fix)) + adam_eps
                )
                new_s[a, rows, cols] = value
                at = pl.ds(pl.multiple_of(a * rank + lax.rem(i, rank // 16) * 16, 16), 16)
                serve[at, cols] = value.astype(jnp.bfloat16)
            return carry

        lax.fori_loop(0, (rank // 16) * (got.shape[2] // 128), block, 0)

    for load in loads:
        load.wait()
    own_gin.wait()
    arrived(gin_s, gin_send, gin_recv)
    update(gin_s, ad_in, new_in_s, serve_in)
    store_in.start()

    every = lax.dot_general(
        hidden, serve_in[...], (((1,), (1,)), ((), ())), preferred_element_type=jnp.float32
    )
    every = every * mask
    inner = every[:, :128]
    for q in range(1, lanes // 128):
        inner += every[:, 128 * q : 128 * q + 128]
    turn = 128
    while turn > rank:
        turn //= 2
        inner += pltpu.roll(inner, turn, 1)
    group = lax.broadcasted_iota(jnp.int32, (8, 128), 1) // rank
    folded = jnp.zeros((8, 128), jnp.float32)
    for q in range(row_count // 8):
        folded += jnp.where(group == q, inner[8 * q : 8 * q + 8, :], 0.0)
    got_inner[me] = folded
    each(lambda p: send_inner(p).start())

    own_gout.wait()
    arrived(gout_s, gout_send, gout_recv)
    update(gout_s, ad_out, new_out_s, serve_out)
    store_out.start()

    def add_part(p):
        send = remote(got_part.at[p], got_part.at[p], part_send.at[p], part_recv.at[p], p)
        send.wait_recv()
        own[...] += got_part[p].astype(jnp.float32)

    each_chip(add_part)

    arrived(got_inner, inner_send, inner_recv)
    inner_sum = got_inner[0]
    for k in range(1, n):
        inner_sum += got_inner[k]
    inner_sum = inner_sum * (1.0 / math.sqrt(FFW))
    pieces = []
    for q in range(row_count // 8):
        piece = jnp.where(group == q, inner_sum, 0.0)
        turn = 128
        while turn > rank:
            turn //= 2
            piece += pltpu.roll(piece, turn, 1)
        pieces.append(piece)
    lifted = jnp.concatenate(pieces, axis=0)
    lifted = jnp.concatenate([lifted] * (lanes // 128), axis=1)
    lifted = (lifted * mask).astype(jnp.bfloat16)
    delta = jnp.dot(lifted, serve_out[...], preferred_element_type=jnp.float32)
    result = own[...] + delta * (1.0 / math.sqrt(rank))
    per = row_count // n
    for j in range(n):
        rows_out[j] = result[per * j : per * j + per, :]
    each(lambda p: send_rows(p).start())
    got_rows[me] = rows_out[me]
    send_tok(mate).wait_send()
    each_chip(lambda p: send_tok(p).wait_send())
    each_chip(lambda p: relay(p).wait_send())
    each(lambda p: send_gin(p).wait_send())
    each(lambda p: send_gout(p).wait_send())
    each_chip(lambda p: send_part(p).wait_send())

    def mate_sent(s, carry):
        send_mate(s).wait_send()
        return carry

    lax.fori_loop(0, half, mate_sent, 0)
    each(lambda p: send_inner(p).wait_send())
    store_in.wait()
    store_out.wait()
    arrived(got_rows, rows_send, rows_recv)
    for j in range(n):
        layer[:, column_block * j : column_block * (j + 1)] = got_rows[j].astype(jnp.bfloat16)
    each(lambda p: send_rows(p).wait_send())


def copy_kernel(*refs):
    sources, targets, sems = refs[:3], refs[3:6], refs[6]
    copies = [
        pltpu.make_async_copy(source, target, sems.at[i])
        for i, (source, target) in enumerate(zip(sources, targets))
    ]
    for copy in copies:
        copy.start()
    for copy in copies:
        copy.wait()


def hand_over(*arrays):
    hbm = pl.BlockSpec(memory_space=pl.ANY)
    return pl.pallas_call(
        copy_kernel,
        out_shape=tuple(jax.ShapeDtypeStruct(a.shape, a.dtype) for a in arrays),
        in_specs=[pl.BlockSpec(memory_space=pltpu.VMEM)] * 3,
        out_specs=(hbm,) * 3,
        scratch_shapes=[pltpu.SemaphoreType.DMA((3,))],
        compiler_params=pltpu.CompilerParams(vmem_limit_bytes=60 * 1024 * 1024),
    )(*arrays)


def fused_shards(
    tokens,
    gate_weight,
    up_weight,
    down_weight,
    grad_in,
    grad_out,
    adapter_in,
    adapter_out,
    moment_in,
    moment_out,
    second_in,
    second_out,
    tenants,
    placement,
    row_slot,
):
    n = lax.axis_size("dev")
    per, model = tokens.shape
    adapters, hidden_block, rank = adapter_in.shape
    column_block = adapter_out.shape[2]
    rows = n * per
    width = model // CHUNKS
    lanes = adapters * rank
    dma = pltpu.SemaphoreType.DMA
    bf16, f32 = jnp.bfloat16, jnp.float32
    vmem, hbm = pl.BlockSpec(memory_space=pltpu.VMEM), pl.BlockSpec(memory_space=pl.ANY)
    smem = pl.BlockSpec(memory_space=pltpu.SMEM)
    layer, new_in, new_out = pl.pallas_call(
        functools.partial(fused_kernel, n),
        out_shape=(
            jax.ShapeDtypeStruct((per, model), bf16),
            jax.ShapeDtypeStruct((adapters, rank, hidden_block), f32),
            jax.ShapeDtypeStruct((adapters, rank, column_block), f32),
        ),
        in_specs=[vmem] + [smem] * 3 + [hbm] * 11,
        out_specs=(vmem, hbm, hbm),
        scratch_shapes=[
            pltpu.VMEM((CHUNKS, width, hidden_block), bf16),
            pltpu.VMEM((CHUNKS, width, hidden_block), bf16),
            pltpu.VMEM((n, hidden_block, column_block), bf16),
            pltpu.VMEM((n, per * CHUNKS, width + 128), bf16),
            pltpu.VMEM((n, rank, hidden_block), bf16),
            pltpu.VMEM((n, rank, column_block), bf16),
            pltpu.VMEM((3, adapters, rank, hidden_block), f32),
            pltpu.VMEM((3, adapters, rank, column_block), f32),
            pltpu.VMEM((adapters, rank, hidden_block), f32),
            pltpu.VMEM((adapters, rank, column_block), f32),
            pltpu.VMEM((lanes, hidden_block), bf16),
            pltpu.VMEM((lanes, column_block), bf16),
            pltpu.VMEM((rows, hidden_block), f32),
            pltpu.VMEM((rows, hidden_block), f32),
            pltpu.VMEM((n // 2, rows, column_block), f32),
            pltpu.VMEM((n // 2, rows, column_block), f32),
            pltpu.VMEM((n, rows, column_block), bf16),
            pltpu.VMEM((rows, column_block), f32),
            pltpu.VMEM((n, rows, column_block), bf16),
            pltpu.VMEM((n * adapters, 128), f32),
            pltpu.VMEM((per * CHUNKS, width + 128), f32),
            pltpu.VMEM((n, 8, 128), f32),
            pltpu.VMEM((n, per, column_block), f32),
            pltpu.VMEM((n, per, column_block), f32),
            dma((2 * CHUNKS + n,)),
            dma((11,)),
        ]
        + [dma((n,))] * 15,
        compiler_params=pltpu.CompilerParams(
            collective_id=0, has_side_effects=True, vmem_limit_bytes=60 * 1024 * 1024
        ),
    )(
        tokens,
        tenants,
        jnp.swapaxes(placement, 0, 1),
        row_slot,
        gate_weight,
        up_weight,
        down_weight,
        jnp.swapaxes(grad_in[0], 0, 1),
        grad_out[0],
        jnp.swapaxes(adapter_in, 1, 2),
        jnp.swapaxes(moment_in, 1, 2),
        jnp.swapaxes(second_in, 1, 2),
        adapter_out,
        moment_out,
        second_out,
    )
    layer, new_in, new_out = hand_over(layer, new_in, new_out)
    return layer, jnp.swapaxes(new_in, 1, 2), new_out


def fits(mesh, tokens, adapter_in, adapter_out):
    n = mesh.shape["dev"]
    per = tokens.shape[0] // (n * mesh.shape["groups"])
    adapters = adapter_in.shape[0] // mesh.shape["groups"]
    rank = adapter_in.shape[2]
    return (
        n % 2 == 0
        and (adapter_in.shape[1] // n) % 128 == 0
        and (adapter_out.shape[2] // n) % 128 == 0
        and per * CHUNKS == 16
        and tokens.shape[1] % (CHUNKS * 128) == 0
        and 128 % rank == 0
        and rank % 16 == 0
        and adapters <= 128
        and (adapters * rank) % 128 == 0
        and n * per == 8 * (128 // rank)
    )


def solution(mesh):
    in_specs = (
        P(("groups", "dev"), None),
        P(None, "dev"),
        P(None, "dev"),
        P("dev", None),
        P(("groups", "dev"), None, None),
        P(("groups", "dev"), None, None),
        P("groups", "dev", None),
        P("groups", None, "dev"),
        P("groups", "dev", None),
        P("groups", None, "dev"),
        P("groups", "dev", None),
        P("groups", None, "dev"),
        P("groups"),
        P("groups", None),
        P(("groups", "dev")),
    )
    out_specs = (P(("groups", "dev"), None), P("groups", "dev", None), P("groups", None, "dev"))

    def program(*args):
        body = fused_shards if fits(mesh, args[0], args[6], args[7]) else shards
        return jax.shard_map(
            body, mesh=mesh, in_specs=in_specs, out_specs=out_specs, check_vma=False
        )(*args)

    return program
```
